32 devices in a mesh: row: 8 (over y, x, core), col: 4 (over z).
Axes of the slice: x: 2, y: 2, z: 4, core: 2. Of those that a mesh axis runs over, the one named last changes fastest.
Arguments:
- sensitivity: bfloat16 [512, 24576], P(('row', 'col')), may hold values from -0.25 to 0.25
- sensor_of_row: int32 [512], P(('row', 'col')), may hold values from 0 to 127
- row_class: int32 [512], P(('row', 'col')), may hold values from 0 to 3
- sensor_precision: float32 [128], replicated, may hold values from 0.25 to 4
- class_weight: float32 [4], replicated, may hold values from 0.25 to 2.5
Outputs:
- hessian: float32 [4, 24576, 6144], P('col', 'row')
The draws below stay inside these ranges and needn't reach their ends.
All inputs are finite; a program needn't handle non-finite values.
Results may differ from the reference program's by a relative error of at most 0.004.
Values may be sent and summed in bfloat16 or wider, within the bound.
A program may use at most 192 MiB of HBM per device.

```python
import math
import jax
import jax.numpy as jnp
from jax import lax

P_SIZE = 24576
NSENS = 128
NCLASS = 4
ROWS = 512
PIECE = 768
N_ROW = 8
N_COL = 4


def place_ends(values, stream_key, least, largest):
    longest = values.shape.index(max(values.shape))
    spots = []
    for shift in (0, 1):
        where = [jax.random.randint(jax.random.fold_in(stream_key, axis), (), 0, length) for axis, length in enumerate(values.shape)]
        where[longest] = (where[longest] + shift) % values.shape[longest]
        spots.append(tuple(where))
    return values.at[spots[0]].set(least).at[spots[1]].set(largest)


def level_of(rng, extent, shards, low, high):
    gain, own = 1.0, jax.random.fold_in(rng, 6)
    for axis_at, shards_of in shards:
        heights = jnp.exp(jax.random.uniform(jax.random.fold_in(own, axis_at), (shards_of,), jnp.float32, low / len(shards), high / len(shards)))
        gain = gain * jnp.repeat(heights, extent[axis_at] // shards_of).reshape([-1 if axis == axis_at else 1 for axis in range(len(extent))])
    return gain


def gaussian(stream_key, dims, deviation, most, shards=(), held_as=jnp.bfloat16):
    array = deviation * jax.random.normal(stream_key, dims, jnp.float32)
    if shards:
        array = array * level_of(stream_key, dims, shards, -0.22, 0.18)
    return jnp.clip(array, -most, most).astype(held_as)


def setup_inputs(seed: int = 0) -> dict:
    streams_of = jax.random.split(jax.random.key(seed), 6)
    return {
        "sensitivity": gaussian(streams_of[0], (ROWS, P_SIZE), ROWS ** -0.5, 0.25, ((0, 32),)),
        "sensor_of_row": place_ends(jax.random.randint(streams_of[1], (ROWS,), 0, NSENS), jax.random.fold_in(streams_of[1], 1), 0, NSENS - 1).astype(jnp.int32),
        "row_class": place_ends(jax.random.randint(streams_of[2], (ROWS,), 0, NCLASS), jax.random.fold_in(streams_of[2], 1), 0, NCLASS - 1).astype(jnp.int32),
        "sensor_precision": jnp.clip(jnp.exp(jax.random.uniform(streams_of[3], (NSENS,), jnp.float32, math.log(0.25), math.log(4.0))), 0.25, 4.0),
        "class_weight": jnp.clip(jnp.exp(jax.random.uniform(streams_of[4], (NCLASS,), jnp.float32, math.log(0.25), math.log(2.5))), 0.25, 2.5),
    }


def reference(sensitivity, sensor_of_row, row_class, sensor_precision, class_weight):
    weight = sensor_precision[sensor_of_row] * class_weight[row_class]
    scaled = (jnp.sqrt(weight)[:, None] * sensitivity.astype(jnp.float32)).astype(jnp.bfloat16)
    grouped = scaled.reshape(ROWS, N_ROW, N_COL, PIECE)
    flipped = scaled.T

    def panel(column):
        chosen = lax.dynamic_index_in_dim(grouped, column, 2, keepdims=False).reshape(ROWS, N_ROW * PIECE)
        return jnp.dot(flipped, chosen, preferred_element_type=jnp.float32)
    return lax.map(panel, jnp.arange(N_COL, dtype=jnp.int32))
```

```python
import functools

import jax
import jax.numpy as jnp
from jax import lax
from jax.experimental import pallas as pl
from jax.experimental.pallas import tpu as pltpu
from jax.sharding import PartitionSpec as P

MESH = pl.DeviceIdType.MESH


def contract(left, right):
    return lax.dot_general(
        left, right, (((0,), (0,)), ((), ())), preferred_element_type=jnp.float32
    )


def scale_rows(sensitivity, sensor_of_row, row_class, sensor_precision, class_weight):
    sensor_match = (
        sensor_of_row[:, None] == jnp.arange(sensor_precision.shape[0], dtype=jnp.int32)[None, :]
    )
    class_match = row_class[:, None] == jnp.arange(class_weight.shape[0], dtype=jnp.int32)[None, :]
    precision = jnp.sum(jnp.where(sensor_match, sensor_precision[None, :], 0.0), axis=1)
    quality = jnp.sum(jnp.where(class_match, class_weight[None, :], 0.0), axis=1)
    return (jnp.sqrt(precision * quality)[:, None] * sensitivity.astype(jnp.float32)).astype(
        jnp.bfloat16
    )


def general(row_count, col_count, scaled):
    piece_width = scaled.shape[1] // (row_count * col_count)
    pieces = lax.all_to_all(scaled, ("row", "col"), split_axis=1, concat_axis=0, tiled=True)
    own_tile = lax.all_gather(pieces, "col", axis=1, tiled=True)
    col_index = lax.axis_index("col")
    my_piece = lax.dynamic_slice_in_dim(own_tile, col_index * piece_width, piece_width, 1)
    return contract(own_tile, lax.all_gather(my_piece, "row", axis=1, tiled=True))


def gather_kernel(
    rows, cols, x_ref, tile_ref, panel_ref,
    own_sem, a_send, a_recv, up_send, down_send, z_recv, keep_sem, p_send, pair_send, p_recv,
):
    r = lax.axis_index("row")
    c = lax.axis_index("col")
    pair = r + 1 - 2 * (r % 2)
    depth = x_ref.shape[0]
    width = x_ref.shape[1] // (rows * cols)
    tile_width = width * cols
    share = depth * rows

    def peer(k):
        return (r + k) % rows

    def other(k):
        return (r + 2 * k) % rows

    barrier = pltpu.get_barrier_semaphore()
    for k in range(1, rows):
        pl.semaphore_signal(barrier, inc=1, device_id=(peer(k), c), device_id_type=MESH)

    @pl.when(c > 0)
    def _():
        pl.semaphore_signal(barrier, inc=1, device_id=(r, c - 1), device_id_type=MESH)

    @pl.when(c < cols - 1)
    def _():
        pl.semaphore_signal(barrier, inc=1, device_id=(r, c + 1), device_id_type=MESH)

    neighbours = (c + cols - 1) // cols + (2 * cols - 2 - c) // cols
    pl.semaphore_wait(barrier, rows - 1 + neighbours)

    def piece_at(q):
        return (q + cols - 1) % cols

    def columns(p):
        return pl.ds(pl.multiple_of(p * width, width), width)

    def deal(k, p):
        to = peer(k)
        return pltpu.make_async_remote_copy(
            src_ref=x_ref.at[:, pl.ds(pl.multiple_of(to * tile_width + p * width, width), width)],
            dst_ref=tile_ref.at[c, pl.ds(pl.multiple_of(r * depth, depth), depth), columns(p)],
            send_sem=a_send.at[k, p],
            recv_sem=a_recv.at[k, p],
            device_id=(to, c),
            device_id_type=MESH,
        )

    def dealt(k, p):
        source = (r + rows - k) % rows
        return pltpu.make_async_remote_copy(
            src_ref=x_ref.at[:, columns(p)],
            dst_ref=tile_ref.at[c, pl.ds(pl.multiple_of(source * depth, depth), depth), columns(p)],
            send_sem=a_send.at[k, p],
            recv_sem=a_recv.at[k, p],
            device_id=(source, c),
            device_id_type=MESH,
        )

    def own_copy():
        return pltpu.make_async_copy(
            x_ref.at[:, pl.ds(pl.multiple_of(r * tile_width, tile_width), tile_width)],
            tile_ref.at[c, pl.ds(pl.multiple_of(r * depth, depth), depth), :],
            own_sem,
        )

    def along(z, p, sem, to):
        block = tile_ref.at[z, :, columns(p)]
        return pltpu.make_async_remote_copy(
            src_ref=block,
            dst_ref=block,
            send_sem=sem.at[z, p],
            recv_sem=z_recv.at[z, p],
            device_id=(r, to),
            device_id_type=MESH,
        )

    def slot(source, z):
        return panel_ref.at[source, pl.ds(pl.multiple_of(z * share, share), share), :]

    def keep(z):
        return pltpu.make_async_copy(tile_ref.at[z, :, columns(c)], slot(r, z), keep_sem.at[z])

    def spread(k, z):
        return pltpu.make_async_remote_copy(
            src_ref=tile_ref.at[z, :, columns(c)],
            dst_ref=slot(r, z),
            send_sem=p_send.at[k, z],
            recv_sem=p_recv.at[r, z],
            device_id=(other(k), c),
            device_id_type=MESH,
        )

    def share_own(z):
        return pltpu.make_async_remote_copy(
            src_ref=tile_ref.at[z, :, columns(c)],
            dst_ref=slot(r, z),
            send_sem=pair_send.at[0, z],
            recv_sem=p_recv.at[r, z],
            device_id=(pair, c),
            device_id_type=MESH,
        )

    def pass_on(k, z):
        source = other(k)
        return pltpu.make_async_remote_copy(
            src_ref=slot(source, z),
            dst_ref=slot(source, z),
            send_sem=pair_send.at[k, z],
            recv_sem=p_recv.at[source, z],
            device_id=(pair, c),
            device_id_type=MESH,
        )

    def start_spread(z):
        for k in range(1, rows // 2):
            spread(k, z).start()
        share_own(z).start()
        keep(z).start()

    def hand_to_pair(z):
        for k in range(1, rows // 2):
            copy = pass_on(k, z)
            copy.wait_recv()
            copy.start()

    own_copy().start()

    def start_deal(q, carry):
        p = piece_at(q)
        for k in range(1, rows):
            deal(k, p).start()
        return carry

    lax.fori_loop(0, cols, start_deal, 0)
    own_copy().wait()

    def first(q, carry):
        p = piece_at(q)
        for k in range(1, rows):
            dealt(k, p).wait_recv()

        @pl.when(c < cols - 1)
        def _():
            along(c, p, up_send, c + 1).start()

        @pl.when(c > 0)
        def _():
            along(c, p, down_send, c - 1).start()

        @pl.when(p == c)
        def _():
            start_spread(c)

        return carry

    lax.fori_loop(0, cols, first, 0)

    for distance in range(1, cols):
        below = c - distance
        above = c + distance

        def step(q, carry, below=below, above=above, distance=distance):
            p = piece_at(q)

            @pl.when(below >= 0)
            def _():
                along(below, p, up_send, c).wait_recv()

                @pl.when(c < cols - 1)
                def _():
                    along(below, p, up_send, c + 1).start()

                @pl.when(p == c)
                def _():
                    start_spread(below)

            @pl.when(above < cols)
            def _():
                along(above, p, down_send, c).wait_recv()

                @pl.when(c > 0)
                def _():
                    along(above, p, down_send, c - 1).start()

                @pl.when(p == c)
                def _():
                    start_spread(above)

            return carry

        lax.fori_loop(0, cols, step, 0)
        if distance == 1:
            hand_to_pair(c)
        else:

            @pl.when(c - distance + 1 >= 0)
            def _(distance=distance):
                hand_to_pair(c - distance + 1)

            @pl.when(c + distance - 1 < cols)
            def _(distance=distance):
                hand_to_pair(c + distance - 1)

    @pl.when(c == cols - 1)
    def _():
        hand_to_pair(0)

    @pl.when(c == 0)
    def _():
        hand_to_pair(cols - 1)

    def finish(z, carry):
        keep(z).wait()
        for k in range(rows // 2):
            source = (pair + 2 * k) % rows
            pltpu.make_async_remote_copy(
                src_ref=slot(source, z),
                dst_ref=slot(source, z),
                send_sem=pair_send.at[k, z],
                recv_sem=p_recv.at[source, z],
                device_id=(pair, c),
                device_id_type=MESH,
            ).wait_recv()
        for k in range(1, rows):
            deal(k, z).wait_send()
        for k in range(1, rows // 2):
            spread(k, z).wait_send()
            pass_on(k, z).wait_send()
        share_own(z).wait_send()

        def sent(p, carry):
            @pl.when((z <= c) & (c < cols - 1))
            def _():
                along(z, p, up_send, c + 1).wait_send()

            @pl.when((z >= c) & (c > 0))
            def _():
                along(z, p, down_send, c - 1).wait_send()

            return carry

        return lax.fori_loop(0, cols, sent, carry)

    lax.fori_loop(0, cols, finish, 0)


def gather(rows, cols, scaled):
    depth, total = scaled.shape
    width = total // (rows * cols)
    dma = pltpu.SemaphoreType.DMA
    return pl.pallas_call(
        functools.partial(gather_kernel, rows, cols),
        out_shape=(
            jax.ShapeDtypeStruct((cols, depth * rows, width * cols), jnp.bfloat16),
            jax.ShapeDtypeStruct((rows, depth * rows * cols, width), jnp.bfloat16),
        ),
        in_specs=[pl.BlockSpec(memory_space=pl.ANY)],
        out_specs=(pl.BlockSpec(memory_space=pl.ANY), pl.BlockSpec(memory_space=pl.ANY)),
        scratch_shapes=[
            dma,
            dma((rows, cols)),
            dma((rows, cols)),
            dma((cols, cols)),
            dma((cols, cols)),
            dma((cols, cols)),
            dma((cols,)),
            dma((rows // 2, cols)),
            dma((rows // 2, cols)),
            dma((rows, cols)),
        ],
        compiler_params=pltpu.CompilerParams(collective_id=0, has_side_effects=True),
    )(scaled)


def product_kernel(tile_ref, panel_ref, out_ref, flipped):
    p = pl.program_id(0)
    i = pl.program_id(1)
    shares, share, width = tile_ref.shape

    @pl.when(p == 0)
    def _():
        for s in range(shares):
            flipped[i, :, s * share : (s + 1) * share] = tile_ref[s].T

    out_ref[0] = jnp.dot(flipped[i], panel_ref[0], preferred_element_type=jnp.float32)


def product(tile, panel):
    shares, share, height = tile.shape
    count, depth, width = panel.shape
    steps = height // width
    return pl.pallas_call(
        product_kernel,
        grid=(count, steps),
        out_shape=jax.ShapeDtypeStruct((1, height, count * width), jnp.float32),
        in_specs=[
            pl.BlockSpec(
                (shares, share, width), lambda p, i: (0, 0, jnp.where(p == 0, i, steps - 1))
            ),
            pl.BlockSpec((1, depth, width), lambda p, i: (p, 0, 0)),
        ],
        out_specs=pl.BlockSpec((1, width, width), lambda p, i: (0, i, p)),
        scratch_shapes=[pltpu.VMEM((steps, width, depth), jnp.bfloat16)],
        compiler_params=pltpu.CompilerParams(vmem_limit_bytes=60 * 2**20),
        cost_estimate=pl.CostEstimate(
            flops=2 * height * count * width * depth,
            bytes_accessed=4 * height * count * width,
            transcendentals=0,
        ),
    )(tile, panel)


def shards(rows, cols, sensitivity, *parameters):
    scaled = scale_rows(sensitivity, *parameters)
    depth, total = scaled.shape
    if rows == 8 and cols == 4 and depth % 16 == 0 and total % (rows * cols * 128) == 0:
        tile, panel = gather(rows, cols, scaled)
        return product(tile, panel)
    return general(rows, cols, scaled)[None]


def solution(mesh):
    return jax.shard_map(
        functools.partial(shards, mesh.shape["row"], mesh.shape["col"]),
        mesh=mesh,
        in_specs=(P(("row", "col"), None), P(("row", "col")), P(("row", "col")), P(), P()),
        out_specs=P("col", "row", None),
        check_vma=False,
    )
```

```python
import functools

import jax
import jax.numpy as jnp
from jax import lax
from jax.experimental import pallas as pl
from jax.experimental.pallas import tpu as pltpu
from jax.sharding import PartitionSpec as P

MESH = pl.DeviceIdType.MESH


def contract(left, right):
    return lax.dot_general(
        left, right, (((0,), (0,)), ((), ())), preferred_element_type=jnp.float32
    )


def scale_rows(sensitivity, sensor_of_row, row_class, sensor_precision, class_weight):
    sensor_match = (
        sensor_of_row[:, None] == jnp.arange(sensor_precision.shape[0], dtype=jnp.int32)[None, :]
    )
    class_match = row_class[:, None] == jnp.arange(class_weight.shape[0], dtype=jnp.int32)[None, :]
    precision = jnp.sum(jnp.where(sensor_match, sensor_precision[None, :], 0.0), axis=1)
    quality = jnp.sum(jnp.where(class_match, class_weight[None, :], 0.0), axis=1)
    return (jnp.sqrt(precision * quality)[:, None] * sensitivity.astype(jnp.float32)).astype(
        jnp.bfloat16
    )


def general(row_count, col_count, scaled):
    piece_width = scaled.shape[1] // (row_count * col_count)
    pieces = lax.all_to_all(scaled, ("row", "col"), split_axis=1, concat_axis=0, tiled=True)
    own_tile = lax.all_gather(pieces, "col", axis=1, tiled=True)
    col_index = lax.axis_index("col")
    my_piece = lax.dynamic_slice_in_dim(own_tile, col_index * piece_width, piece_width, 1)
    return contract(own_tile, lax.all_gather(my_piece, "row", axis=1, tiled=True))


def gather_kernel(
    rows, cols, x_ref, tile_ref, panel_ref,
    own_sem, a_send, a_recv, up_send, down_send, z_recv, keep_sem, p_send, pair_send, p_recv,
):
    r = lax.axis_index("row")
    c = lax.axis_index("col")
    pair = r + 1 - 2 * (r % 2)
    depth = x_ref.shape[0]
    width = x_ref.shape[1] // (rows * cols)
    tile_width = width * cols
    share = depth * rows

    def peer(k):
        return (r + k) % rows

    def other(k):
        return (r + 2 * k) % rows

    barrier = pltpu.get_barrier_semaphore()
    for k in range(1, rows):
        pl.semaphore_signal(barrier, inc=1, device_id=(peer(k), c), device_id_type=MESH)

    @pl.when(c > 0)
    def _():
        pl.semaphore_signal(barrier, inc=1, device_id=(r, c - 1), device_id_type=MESH)

    @pl.when(c < cols - 1)
    def _():
        pl.semaphore_signal(barrier, inc=1, device_id=(r, c + 1), device_id_type=MESH)

    neighbours = (c + cols - 1) // cols + (2 * cols - 2 - c) // cols
    pl.semaphore_wait(barrier, rows - 1 + neighbours)

    def piece_at(q):
        return (q + cols - 1) % cols

    def columns(p):
        return pl.ds(pl.multiple_of(p * width, width), width)

    def deal(k, p):
        to = peer(k)
        return pltpu.make_async_remote_copy(
            src_ref=x_ref.at[:, pl.ds(pl.multiple_of(to * tile_width + p * width, width), width)],
            dst_ref=tile_ref.at[c, pl.ds(pl.multiple_of(r * depth, depth), depth), columns(p)],
            send_sem=a_send.at[k, p],
            recv_sem=a_recv.at[k, p],
            device_id=(to, c),
            device_id_type=MESH,
        )

    def dealt(k, p):
        source = (r + rows - k) % rows
        return pltpu.make_async_remote_copy(
            src_ref=x_ref.at[:, columns(p)],
            dst_ref=tile_ref.at[c, pl.ds(pl.multiple_of(source * depth, depth), depth), columns(p)],
            send_sem=a_send.at[k, p],
            recv_sem=a_recv.at[k, p],
            device_id=(source, c),
            device_id_type=MESH,
        )

    def own_copy():
        return pltpu.make_async_copy(
            x_ref.at[:, pl.ds(pl.multiple_of(r * tile_width, tile_width), tile_width)],
            tile_ref.at[c, pl.ds(pl.multiple_of(r * depth, depth), depth), :],
            own_sem,
        )

    def along(z, p, sem, to):
        block = tile_ref.at[z, :, columns(p)]
        return pltpu.make_async_remote_copy(
            src_ref=block,
            dst_ref=block,
            send_sem=sem.at[z, p],
            recv_sem=z_recv.at[z, p],
            device_id=(r, to),
            device_id_type=MESH,
        )

    def slot(source, z):
        return panel_ref.at[source, pl.ds(pl.multiple_of(z * share, share), share), :]

    def keep(z):
        return pltpu.make_async_copy(tile_ref.at[z, :, columns(c)], slot(r, z), keep_sem.at[z])

    def spread(k, z):
        return pltpu.make_async_remote_copy(
            src_ref=tile_ref.at[z, :, columns(c)],
            dst_ref=slot(r, z),
            send_sem=p_send.at[k, z],
            recv_sem=p_recv.at[r, z],
            device_id=(other(k), c),
            device_id_type=MESH,
        )

    def share_own(z):
        return pltpu.make_async_remote_copy(
            src_ref=tile_ref.at[z, :, columns(c)],
            dst_ref=slot(r, z),
            send_sem=pair_send.at[0, z],
            recv_sem=p_recv.at[r, z],
            device_id=(pair, c),
            device_id_type=MESH,
        )

    def pass_on(k, z):
        source = other(k)
        return pltpu.make_async_remote_copy(
            src_ref=slot(source, z),
            dst_ref=slot(source, z),
            send_sem=pair_send.at[k, z],
            recv_sem=p_recv.at[source, z],
            device_id=(pair, c),
            device_id_type=MESH,
        )

    def start_spread(z):
        for k in range(1, rows // 2):
            spread(k, z).start()
        share_own(z).start()
        keep(z).start()

    def hand_to_pair(z):
        for k in range(1, rows // 2):
            copy = pass_on(k, z)
            copy.wait_recv()
            copy.start()

    own_copy().start()

    def start_deal(q, carry):
        p = piece_at(q)
        for k in range(1, rows):
            deal(k, p).start()
        return carry

    lax.fori_loop(0, cols, start_deal, 0)
    own_copy().wait()

    def first(q, carry):
        p = piece_at(q)
        for k in range(1, rows):
            dealt(k, p).wait_recv()

        @pl.when(c < cols - 1)
        def _():
            along(c, p, up_send, c + 1).start()

        @pl.when(c > 0)
        def _():
            along(c, p, down_send, c - 1).start()

        @pl.when(p == c)
        def _():
            start_spread(c)

        return carry

    lax.fori_loop(0, cols, first, 0)

    for distance in range(1, cols):
        below = c - distance
        above = c + distance

        def step(q, carry, below=below, above=above, distance=distance):
            p = piece_at(q)

            @pl.when(below >= 0)
            def _():
                along(below, p, up_send, c).wait_recv()

                @pl.when(c < cols - 1)
                def _():
                    along(below, p, up_send, c + 1).start()

                @pl.when(p == c)
                def _():
                    start_spread(below)

            @pl.when(above < cols)
            def _():
                along(above, p, down_send, c).wait_recv()

                @pl.when(c > 0)
                def _():
                    along(above, p, down_send, c - 1).start()

                @pl.when(p == c)
                def _():
                    start_spread(above)

            return carry

        lax.fori_loop(0, cols, step, 0)
        if distance == 1:
            hand_to_pair(c)
        else:

            @pl.when(c - distance + 1 >= 0)
            def _(distance=distance):
                hand_to_pair(c - distance + 1)

            @pl.when(c + distance - 1 < cols)
            def _(distance=distance):
                hand_to_pair(c + distance - 1)

    @pl.when(c == cols - 1)
    def _():
        hand_to_pair(0)

    @pl.when(c == 0)
    def _():
        hand_to_pair(cols - 1)

    def finish(z, carry):
        keep(z).wait()
        for k in range(rows // 2):
            source = (pair + 2 * k) % rows
            pltpu.make_async_remote_copy(
                src_ref=slot(source, z),
                dst_ref=slot(source, z),
                send_sem=pair_send.at[k, z],
                recv_sem=p_recv.at[source, z],
                device_id=(pair, c),
                device_id_type=MESH,
            ).wait_recv()
        for k in range(1, rows):
            deal(k, z).wait_send()
        for k in range(1, rows // 2):
            spread(k, z).wait_send()
            pass_on(k, z).wait_send()
        share_own(z).wait_send()

        def sent(p, carry):
            @pl.when((z <= c) & (c < cols - 1))
            def _():
                along(z, p, up_send, c + 1).wait_send()

            @pl.when((z >= c) & (c > 0))
            def _():
                along(z, p, down_send, c - 1).wait_send()

            return carry

        return lax.fori_loop(0, cols, sent, carry)

    lax.fori_loop(0, cols, finish, 0)


def gather(rows, cols, scaled):
    depth, total = scaled.shape
    width = total // (rows * cols)
    dma = pltpu.SemaphoreType.DMA
    return pl.pallas_call(
        functools.partial(gather_kernel, rows, cols),
        out_shape=(
            jax.ShapeDtypeStruct((cols, depth * rows, width * cols), jnp.bfloat16),
            jax.ShapeDtypeStruct((rows, depth * rows * cols, width), jnp.bfloat16),
        ),
        in_specs=[pl.BlockSpec(memory_space=pl.ANY)],
        out_specs=(pl.BlockSpec(memory_space=pl.ANY), pl.BlockSpec(memory_space=pl.ANY)),
        scratch_shapes=[
            dma,
            dma((rows, cols)),
            dma((rows, cols)),
            dma((cols, cols)),
            dma((cols, cols)),
            dma((cols, cols)),
            dma((cols,)),
            dma((rows // 2, cols)),
            dma((rows // 2, cols)),
            dma((rows, cols)),
        ],
        compiler_params=pltpu.CompilerParams(collective_id=0, has_side_effects=True),
    )(scaled)


def product_kernel(tile_ref, panel_ref, out_ref, flipped):
    p = pl.program_id(0)
    shares, share, height = tile_ref.shape

    @pl.when(p == 0)
    def _():
        for s in range(shares):
            flipped[:, s * share : (s + 1) * share] = tile_ref[s].T

    out_ref[0] = jnp.dot(flipped[...], panel_ref[0], preferred_element_type=jnp.float32)


def product(tile, panel):
    shares, share, height = tile.shape
    count, depth, width = panel.shape
    return pl.pallas_call(
        product_kernel,
        grid=(count,),
        out_shape=jax.ShapeDtypeStruct((1, height, count * width), jnp.float32),
        in_specs=[
            pl.BlockSpec((shares, share, height), lambda p: (0, 0, 0)),
            pl.BlockSpec((1, depth, width), lambda p: (p, 0, 0)),
        ],
        out_specs=pl.BlockSpec((1, height, width), lambda p: (0, 0, p)),
        scratch_shapes=[pltpu.VMEM((height, depth), jnp.bfloat16)],
        compiler_params=pltpu.CompilerParams(vmem_limit_bytes=60 * 2**20),
        cost_estimate=pl.CostEstimate(
            flops=2 * height * count * width * depth,
            bytes_accessed=4 * height * count * width,
            transcendentals=0,
        ),
    )(tile, panel)


def shards(rows, cols, sensitivity, *parameters):
    scaled = scale_rows(sensitivity, *parameters)
    depth, total = scaled.shape
    if rows == 8 and cols == 4 and depth % 16 == 0 and total % (rows * cols * 128) == 0:
        tile, panel = gather(rows, cols, scaled)
        return product(tile, panel)
    return general(rows, cols, scaled)[None]


def solution(mesh):
    return jax.shard_map(
        functools.partial(shards, mesh.shape["row"], mesh.shape["col"]),
        mesh=mesh,
        in_specs=(P(("row", "col"), None), P(("row", "col")), P(("row", "col")), P(), P()),
        out_specs=P("col", "row", None),
        check_vma=False,
    )
```

```python
import functools

import jax
import jax.numpy as jnp
from jax import lax
from jax.experimental import pallas as pl
from jax.experimental.pallas import tpu as pltpu
from jax.sharding import PartitionSpec as P

MESH = pl.DeviceIdType.MESH


def contract(left, right):
    return lax.dot_general(
        left, right, (((0,), (0,)), ((), ())), preferred_element_type=jnp.float32
    )


def scale_rows(sensitivity, sensor_of_row, row_class, sensor_precision, class_weight):
    sensor_match = (
        sensor_of_row[:, None] == jnp.arange(sensor_precision.shape[0], dtype=jnp.int32)[None, :]
    )
    class_match = row_class[:, None] == jnp.arange(class_weight.shape[0], dtype=jnp.int32)[None, :]
    precision = jnp.sum(jnp.where(sensor_match, sensor_precision[None, :], 0.0), axis=1)
    quality = jnp.sum(jnp.where(class_match, class_weight[None, :], 0.0), axis=1)
    return (jnp.sqrt(precision * quality)[:, None] * sensitivity.astype(jnp.float32)).astype(
        jnp.bfloat16
    )


def general(row_count, col_count, scaled):
    piece_width = scaled.shape[1] // (row_count * col_count)
    pieces = lax.all_to_all(scaled, ("row", "col"), split_axis=1, concat_axis=0, tiled=True)
    own_tile = lax.all_gather(pieces, "col", axis=1, tiled=True)
    col_index = lax.axis_index("col")
    my_piece = lax.dynamic_slice_in_dim(own_tile, col_index * piece_width, piece_width, 1)
    return contract(own_tile, lax.all_gather(my_piece, "row", axis=1, tiled=True))


def gather_kernel(
    rows, cols, raw_ref, sensor_ref, class_ref, precision_ref, quality_ref, tile_ref, panel_ref,
    x_ref, own_sem, a_send, a_recv, up_send, down_send, z_recv, keep_sem, p_send, pair_send, p_recv,
):
    r = lax.axis_index("row")
    c = lax.axis_index("col")
    pair = r + 1 - 2 * (r % 2)
    depth = x_ref.shape[0]
    width = x_ref.shape[1] // (rows * cols)
    tile_width = width * cols
    share = depth * rows

    def peer(k):
        return (r + k) % rows

    def other(k):
        return (r + 2 * k) % rows

    barrier = pltpu.get_barrier_semaphore()
    for k in range(1, rows):
        pl.semaphore_signal(barrier, inc=1, device_id=(peer(k), c), device_id_type=MESH)

    @pl.when(c > 0)
    def _():
        pl.semaphore_signal(barrier, inc=1, device_id=(r, c - 1), device_id_type=MESH)

    @pl.when(c < cols - 1)
    def _():
        pl.semaphore_signal(barrier, inc=1, device_id=(r, c + 1), device_id_type=MESH)

    def pick(index_ref, table_ref):
        spots = lax.broadcasted_iota(jnp.int32, (depth, table_ref.shape[1]), 1)
        return jnp.sum(
            jnp.where(index_ref[...] == spots, table_ref[...], 0.0), axis=1, keepdims=True
        )

    root = jnp.sqrt(pick(sensor_ref, precision_ref) * pick(class_ref, quality_ref))

    def scale(i, carry):
        part = pl.ds(pl.multiple_of(i * width, width), width)
        x_ref[:, part] = (root * raw_ref[:, part].astype(jnp.float32)).astype(jnp.bfloat16)
        return carry

    lax.fori_loop(0, rows * cols, scale, 0)

    neighbours = (c + cols - 1) // cols + (2 * cols - 2 - c) // cols
    pl.semaphore_wait(barrier, rows - 1 + neighbours)

    def piece_at(q):
        return (q + cols - 1) % cols

    def columns(p):
        return pl.ds(pl.multiple_of(p * width, width), width)

    def deal(k, p):
        to = peer(k)
        return pltpu.make_async_remote_copy(
            src_ref=x_ref.at[:, pl.ds(pl.multiple_of(to * tile_width + p * width, width), width)],
            dst_ref=tile_ref.at[c, pl.ds(pl.multiple_of(r * depth, depth), depth), columns(p)],
            send_sem=a_send.at[k, p],
            recv_sem=a_recv.at[k, p],
            device_id=(to, c),
            device_id_type=MESH,
        )

    def dealt(k, p):
        source = (r + rows - k) % rows
        return pltpu.make_async_remote_copy(
            src_ref=x_ref.at[:, columns(p)],
            dst_ref=tile_ref.at[c, pl.ds(pl.multiple_of(source * depth, depth), depth), columns(p)],
            send_sem=a_send.at[k, p],
            recv_sem=a_recv.at[k, p],
            device_id=(source, c),
            device_id_type=MESH,
        )

    def own_copy():
        return pltpu.make_async_copy(
            x_ref.at[:, pl.ds(pl.multiple_of(r * tile_width, tile_width), tile_width)],
            tile_ref.at[c, pl.ds(pl.multiple_of(r * depth, depth), depth), :],
            own_sem,
        )

    def along(z, p, sem, to):
        block = tile_ref.at[z, :, columns(p)]
        return pltpu.make_async_remote_copy(
            src_ref=block,
            dst_ref=block,
            send_sem=sem.at[z, p],
            recv_sem=z_recv.at[z, p],
            device_id=(r, to),
            device_id_type=MESH,
        )

    def slot(source, z):
        return panel_ref.at[source, pl.ds(pl.multiple_of(z * share, share), share), :]

    def keep(z):
        return pltpu.make_async_copy(tile_ref.at[z, :, columns(c)], slot(r, z), keep_sem.at[z])

    def spread(k, z):
        return pltpu.make_async_remote_copy(
            src_ref=tile_ref.at[z, :, columns(c)],
            dst_ref=slot(r, z),
            send_sem=p_send.at[k, z],
            recv_sem=p_recv.at[r, z],
            device_id=(other(k), c),
            device_id_type=MESH,
        )

    def share_own(z):
        return pltpu.make_async_remote_copy(
            src_ref=tile_ref.at[z, :, columns(c)],
            dst_ref=slot(r, z),
            send_sem=pair_send.at[0, z],
            recv_sem=p_recv.at[r, z],
            device_id=(pair, c),
            device_id_type=MESH,
        )

    def pass_on(k, z):
        source = other(k)
        return pltpu.make_async_remote_copy(
            src_ref=slot(source, z),
            dst_ref=slot(source, z),
            send_sem=pair_send.at[k, z],
            recv_sem=p_recv.at[source, z],
            device_id=(pair, c),
            device_id_type=MESH,
        )

    def start_spread(z):
        for k in range(1, rows // 2):
            spread(k, z).start()
        share_own(z).start()
        keep(z).start()

    def hand_to_pair(z):
        for k in range(1, rows // 2):
            copy = pass_on(k, z)
            copy.wait_recv()
            copy.start()

    own_copy().start()

    def start_deal(q, carry):
        p = piece_at(q)
        for k in range(1, rows):
            deal(k, p).start()
        return carry

    lax.fori_loop(0, cols, start_deal, 0)
    own_copy().wait()

    def first(q, carry):
        p = piece_at(q)
        for k in range(1, rows):
            dealt(k, p).wait_recv()

        @pl.when(c < cols - 1)
        def _():
            along(c, p, up_send, c + 1).start()

        @pl.when(c > 0)
        def _():
            along(c, p, down_send, c - 1).start()

        @pl.when(p == c)
        def _():
            start_spread(c)

        return carry

    lax.fori_loop(0, cols, first, 0)

    for distance in range(1, cols):
        below = c - distance
        above = c + distance

        def step(q, carry, below=below, above=above, distance=distance):
            p = piece_at(q)

            @pl.when(below >= 0)
            def _():
                along(below, p, up_send, c).wait_recv()

                @pl.when(c < cols - 1)
                def _():
                    along(below, p, up_send, c + 1).start()

                @pl.when(p == c)
                def _():
                    start_spread(below)

            @pl.when(above < cols)
            def _():
                along(above, p, down_send, c).wait_recv()

                @pl.when(c > 0)
                def _():
                    along(above, p, down_send, c - 1).start()

                @pl.when(p == c)
                def _():
                    start_spread(above)

            return carry

        lax.fori_loop(0, cols, step, 0)
        if distance == 1:
            hand_to_pair(c)
        else:

            @pl.when(c - distance + 1 >= 0)
            def _(distance=distance):
                hand_to_pair(c - distance + 1)

            @pl.when(c + distance - 1 < cols)
            def _(distance=distance):
                hand_to_pair(c + distance - 1)

    @pl.when(c == cols - 1)
    def _():
        hand_to_pair(0)

    @pl.when(c == 0)
    def _():
        hand_to_pair(cols - 1)

    def finish(z, carry):
        keep(z).wait()
        for k in range(rows // 2):
            source = (pair + 2 * k) % rows
            pltpu.make_async_remote_copy(
                src_ref=slot(source, z),
                dst_ref=slot(source, z),
                send_sem=pair_send.at[k, z],
                recv_sem=p_recv.at[source, z],
                device_id=(pair, c),
                device_id_type=MESH,
            ).wait_recv()
        for k in range(1, rows):
            deal(k, z).wait_send()
        for k in range(1, rows // 2):
            spread(k, z).wait_send()
            pass_on(k, z).wait_send()
        share_own(z).wait_send()

        def sent(p, carry):
            @pl.when((z <= c) & (c < cols - 1))
            def _():
                along(z, p, up_send, c + 1).wait_send()

            @pl.when((z >= c) & (c > 0))
            def _():
                along(z, p, down_send, c - 1).wait_send()

            return carry

        return lax.fori_loop(0, cols, sent, carry)

    lax.fori_loop(0, cols, finish, 0)


def gather(rows, cols, sensitivity, sensor_of_row, row_class, sensor_precision, class_weight):
    depth, total = sensitivity.shape
    width = total // (rows * cols)
    dma = pltpu.SemaphoreType.DMA
    return pl.pallas_call(
        functools.partial(gather_kernel, rows, cols),
        out_shape=(
            jax.ShapeDtypeStruct((cols, depth * rows, width * cols), jnp.bfloat16),
            jax.ShapeDtypeStruct((rows, depth * rows * cols, width), jnp.bfloat16),
        ),
        in_specs=[pl.BlockSpec(memory_space=pltpu.VMEM)] * 5,
        out_specs=(pl.BlockSpec(memory_space=pl.ANY), pl.BlockSpec(memory_space=pl.ANY)),
        scratch_shapes=[
            pltpu.VMEM((depth, total), jnp.bfloat16),
            dma,
            dma((rows, cols)),
            dma((rows, cols)),
            dma((cols, cols)),
            dma((cols, cols)),
            dma((cols, cols)),
            dma((cols,)),
            dma((rows // 2, cols)),
            dma((rows // 2, cols)),
            dma((rows, cols)),
        ],
        compiler_params=pltpu.CompilerParams(
            collective_id=0, has_side_effects=True, vmem_limit_bytes=58 * 2**20
        ),
    )(
        sensitivity,
        sensor_of_row[:, None],
        row_class[:, None],
        sensor_precision[None, :],
        class_weight[None, :],
    )


def product_kernel(tile_ref, panel_ref, out_ref, flipped):
    p = pl.program_id(0)
    shares, share, height = tile_ref.shape

    @pl.when(p == 0)
    def _():
        for s in range(shares):
            flipped[:, s * share : (s + 1) * share] = tile_ref[s].T

    out_ref[0] = jnp.dot(flipped[...], panel_ref[0], preferred_element_type=jnp.float32)


def product(tile, panel):
    shares, share, height = tile.shape
    count, depth, width = panel.shape
    return pl.pallas_call(
        product_kernel,
        grid=(count,),
        out_shape=jax.ShapeDtypeStruct((1, height, count * width), jnp.float32),
        in_specs=[
            pl.BlockSpec((shares, share, height), lambda p: (0, 0, 0)),
            pl.BlockSpec((1, depth, width), lambda p: (p, 0, 0)),
        ],
        out_specs=pl.BlockSpec((1, height, width), lambda p: (0, 0, p)),
        scratch_shapes=[pltpu.VMEM((height, depth), jnp.bfloat16)],
        compiler_params=pltpu.CompilerParams(vmem_limit_bytes=60 * 2**20),
        cost_estimate=pl.CostEstimate(
            flops=2 * height * count * width * depth,
            bytes_accessed=4 * height * count * width,
            transcendentals=0,
        ),
    )(tile, panel)


def shards(rows, cols, sensitivity, *parameters):
    depth, total = sensitivity.shape
    if rows == 8 and cols == 4 and depth % 16 == 0 and total % (rows * cols * 128) == 0:
        tile, panel = gather(rows, cols, sensitivity, *parameters)
        return product(tile, panel)
    return general(rows, cols, scale_rows(sensitivity, *parameters))[None]


def solution(mesh):
    return jax.shard_map(
        functools.partial(shards, mesh.shape["row"], mesh.shape["col"]),
        mesh=mesh,
        in_specs=(P(("row", "col"), None), P(("row", "col")), P(("row", "col")), P(), P()),
        out_specs=P("col", "row", None),
        check_vma=False,
    )
```
